256 devices in a mesh: band: 16 (over x, z_hi), tx: 8 (over y, z_lo), ty: 2 (over core).
Axes of the slice: x: 4, y: 4, z: 8 (z_hi: 4, z_lo: 2; z = z_hi * 2 + z_lo), core: 2. Of those that a mesh axis runs over, the one named last changes fastest.
Arguments:
- orbitals: bfloat16 [2048, 3, 128, 256], P('band', None, 'tx', 'ty'), may hold values from -6 to 6
- potential: float32 [3, 128, 256], P(None, 'tx', 'ty'), may hold values from 0.5 to 3
- pair_masks: int32 [2], replicated, may hold values from 1 to 15, as said below
Outputs:
- gram_pairs: float32 [2, 2048, 128], P(None, 'band')
- ham_pairs: float32 [2, 2048, 128], P(None, 'band')
The draws below stay inside these ranges and needn't reach their ends.
Inputs may be any that keep to these rules, and one draw needn't show every extreme that they name: The 2 values are distinct; in round r band group g is paired with group g XOR pair_masks[r].
All inputs are finite; a program needn't handle non-finite values.
Results may differ from the reference program's by a relative error of at most 0.0029.
Values may be sent and summed in bfloat16 or wider, within the bound.
No kernel may reach another device: no remote copies, remote signals or barrier semaphores. Data moves between devices by JAX's collectives and lax.ppermute only.
A program may use at most 128 MiB of HBM per device.

```python
import jax
import jax.numpy as jnp
from jax import lax

BAND_DEV = 128
NZ = 3
ROUNDS = 2
GROUPS = 16
ORBITALS = 2048
NX = 128
NY = 256


def draw_pair_masks(key, part):
    key = jax.random.fold_in(key, 7)
    spare_key, choose_key = jax.random.split(key)
    other_mask = jax.random.randint(spare_key, (), 1, GROUPS - 1, dtype=jnp.int32)
    choose = jax.random.randint(choose_key, (), 0, 2, dtype=jnp.int32)
    top_mask = jnp.int32(GROUPS - 1)
    first_mask = jnp.where(choose == 1, other_mask, top_mask)
    second_mask = jnp.where(choose == 1, top_mask, other_mask)
    return jnp.stack([first_mask, second_mask]).astype(jnp.int32)


def block_levels(stream_key, extent, cuts, low, largest):
    factor_of, own = 1.0, jax.random.fold_in(stream_key, 6)
    for dim, parts in cuts:
        heights = jnp.exp(jax.random.uniform(jax.random.fold_in(own, dim), (parts,), jnp.float32, low / len(cuts), largest / len(cuts)))
        factor_of = factor_of * jnp.repeat(heights, extent[dim] // parts).reshape([-1 if axis == dim else 1 for axis in range(len(extent))])
    return factor_of


def scatter_about(stream_key, extent, spread, most, pieces=(), held_as=jnp.bfloat16):
    values = jax.random.normal(stream_key, extent, jnp.float32) * spread
    if len(pieces) > 0:
        values = block_levels(stream_key, extent, pieces, -0.22, 0.18) * values
    return jnp.clip(values, min=-most, max=most).astype(held_as)


def setup_inputs(seed: int = 0) -> dict:
    arg_keys = jax.random.split(jax.random.key(seed), 4)
    return {
        "orbitals": scatter_about(arg_keys[0], (ORBITALS, NZ, NX, NY), 1.0, 6.0, ((0, 16), (2, 8), (3, 2))),
        "potential": jnp.clip(0.5 + 2.5 * jax.random.uniform(arg_keys[1], (NZ, NX, NY), jnp.float32) ** block_levels(arg_keys[1], (NZ, NX, NY), ((1, 8), (2, 2)), -0.2, 0.2), 0.5, 3.0),
        "pair_masks": draw_pair_masks(jax.random.fold_in(arg_keys[3], 71), 0),
    }


COEFFS = (-5369.0 / 1800.0, 12.0 / 7.0, -15.0 / 56.0, 10.0 / 189.0, -1.0 / 112.0, 2.0 / 1925.0, -1.0 / 16632.0)


def laplacian(center):
    summed = 3.0 * COEFFS[0] * center
    for axis_id in (1, 2, 3):
        for offset in range(1, 7):
            summed = summed + COEFFS[offset] * (jnp.roll(center, offset, axis_id) + jnp.roll(center, -offset, axis_id))
    return summed


def reference(orbitals, potential, pair_masks):
    norm_scale = float(NZ * NX * NY) ** -0.5

    def one_group(group_id):
        first_row = (group_id * BAND_DEV).astype(jnp.int32)
        own_block = lax.dynamic_slice_in_dim(orbitals, first_row, BAND_DEV, 0)
        center = own_block.astype(jnp.float32)
        applied = (-0.5 * laplacian(center) + potential[None] * center).astype(jnp.bfloat16)
        stacked = jnp.concatenate([own_block, applied], 0).reshape(2 * BAND_DEV, -1)
        blocks = []
        for round_id in range(ROUNDS):
            partner = jnp.bitwise_xor(group_id, pair_masks[round_id]).astype(jnp.int32)
            partner_block = lax.dynamic_slice_in_dim(orbitals, (partner * BAND_DEV).astype(jnp.int32), BAND_DEV, 0)
            partner_block = partner_block.reshape(BAND_DEV, -1)
            blocks.append(lax.dot_general(stacked, partner_block, (((1,), (1,)), ((), ())), preferred_element_type=jnp.float32))
        return jnp.stack(blocks)

    result = lax.map(one_group, jnp.arange(GROUPS, dtype=jnp.int32)) * norm_scale
    gram_pairs = result[:, :, :BAND_DEV].transpose(1, 0, 2, 3).reshape(ROUNDS, ORBITALS, BAND_DEV)
    ham_pairs = result[:, :, BAND_DEV:].transpose(1, 0, 2, 3).reshape(ROUNDS, ORBITALS, BAND_DEV)
    return gram_pairs, ham_pairs
```

```python
import jax
import jax.numpy as jnp
import numpy as np
from jax import lax
from jax.experimental import pallas as pl
from jax.experimental.pallas import tpu as pltpu
from jax.sharding import PartitionSpec as P

COEFFS = (
    -5369.0 / 1800.0,
    12.0 / 7.0,
    -15.0 / 56.0,
    10.0 / 189.0,
    -1.0 / 112.0,
    2.0 / 1925.0,
    -1.0 / 16632.0,
)
RADIUS = 6
GROUPS = 16


def parity(value):
    return bin(value).count("1") & 1


def sending_bits(low, high):
    order = [1, 2] + ([11, 7, 13, 14] if (low & 3 == 0) != (high & 3 == 0) else []) + list(range(1, 16))
    for bits in order:
        if parity(bits & low) and parity(bits & high):
            return bits
    raise ValueError("equal masks")


def plans():
    found = []
    for high in range(2, GROUPS):
        for low in range(1, high):
            bits = sending_bits(low, high)
            forth = [(g, g ^ (high if parity(bits & g) else low)) for g in range(GROUPS)]
            found.append((bits, forth))
    return found


def stencil_y_matrix(cells, period):
    matrix = np.zeros((period, cells), np.float64)
    for cell in range(cells):
        for offset in range(1, RADIUS + 1):
            matrix[(cell + offset) % period, cell] += -0.5 * COEFFS[offset]
            matrix[(cell - offset) % period, cell] += -0.5 * COEFFS[offset]
    high = matrix.astype(jnp.bfloat16)
    low = (matrix - high.astype(np.float64)).astype(jnp.bfloat16)
    return np.concatenate([high, low], 1)


def stencil_kernel(own_ref, before_ref, after_ref, other_ref, potential_ref, matrix_ref, applied_ref, wide_ref):
    planes, x_cells, _, y_cells = own_ref.shape
    beta = COEFFS[1] + COEFFS[2] + COEFFS[4] + COEFFS[5]
    kappa = -0.5 * (3.0 * COEFFS[0] + 2.0 * COEFFS[3] + 2.0 * COEFFS[6] - beta)

    def widen(x, carry):
        for z in range(planes):
            wide_ref[z, RADIUS + x] = own_ref[z, x].astype(jnp.float32)
        return carry

    def widen_sides(x, carry):
        for z in range(planes):
            wide_ref[z, x] = before_ref[z, x].astype(jnp.float32)
            wide_ref[z, RADIUS + x_cells + x] = after_ref[z, x].astype(jnp.float32)
        return carry

    lax.fori_loop(0, x_cells, widen, 0)
    lax.fori_loop(0, RADIUS, widen_sides, 0)
    matrix = matrix_ref[...]

    def step(x, carry):
        centers = [wide_ref[z, RADIUS + x] for z in range(planes)]
        plane_sum = (-0.5 * beta) * (centers[0] + centers[1] + centers[2])
        for z in range(planes):
            ring = jnp.concatenate([own_ref[z, x], other_ref[z, x]], 1)
            along_y = jnp.dot(ring, matrix, preferred_element_type=jnp.float32)
            total = plane_sum + (potential_ref[z, x] + kappa) * centers[z]
            for offset in range(1, RADIUS + 1):
                total = total + (-0.5 * COEFFS[offset]) * (
                    wide_ref[z, RADIUS + x + offset] + wide_ref[z, RADIUS + x - offset]
                )
            total = total + (along_y[:, :y_cells] + along_y[:, y_cells:])
            applied_ref[z, x] = total.astype(jnp.bfloat16)
        return carry

    lax.fori_loop(0, x_cells, step, 0)


def blocks_kernel(norm_scale, own_ref, applied_ref, partner_ref, out_ref):
    planes, x_cells, bands, _ = own_ref.shape
    gram = jnp.zeros((bands, bands), jnp.float32)
    ham = jnp.zeros((bands, bands), jnp.float32)
    for z in range(planes):
        for x in range(0, x_cells, 2):
            pair = lambda ref: jnp.concatenate([ref[z, x], ref[z, x + 1]], 1)
            partner = pair(partner_ref)
            dims = (((1,), (1,)), ((), ()))
            gram += lax.dot_general(pair(own_ref), partner, dims, preferred_element_type=jnp.float32)
            ham += lax.dot_general(pair(applied_ref), partner, dims, preferred_element_type=jnp.float32)
    out_ref[0] = gram * norm_scale
    out_ref[1] = ham * norm_scale


def vmem(count):
    return [pl.BlockSpec(memory_space=pltpu.VMEM)] * count


def body(orbitals, potential, pair_masks):
    bands, planes, x_cells, y_cells = orbitals.shape
    tx_count = lax.axis_size("tx")
    group = lax.axis_index("band")
    core = lax.axis_index("ty")
    norm_scale = float(planes * x_cells * y_cells * tx_count * lax.axis_size("ty")) ** -0.5

    low, high = jnp.min(pair_masks), jnp.max(pair_masks)
    plan_index = (high - 1) * (high - 2) // 2 + low - 1
    plan_list = plans()

    own = jnp.transpose(orbitals, (1, 2, 0, 3))
    other_core = [(0, 1), (1, 0)]
    ring_up = [(i, (i + 1) % tx_count) for i in range(tx_count)]
    ring_down = [((i + 1) % tx_count, i) for i in range(tx_count)]
    before = lax.ppermute(own[:, x_cells - RADIUS :], "tx", ring_up)
    after = lax.ppermute(own[:, :RADIUS], "tx", ring_down)
    other = lax.ppermute(own, "ty", other_core)

    def forth(plan):
        return lambda value: (lax.ppermute(value, "band", plan[1]), jnp.int32(plan[0]))

    def back(plan):
        return lambda value: lax.ppermute(value, "band", [(t, s) for s, t in plan[1]])

    partner, bits = lax.switch(plan_index, [forth(plan) for plan in plan_list], own)
    later = lax.population_count(jnp.bitwise_and(bits, group)) & 1

    matrix = jnp.asarray(stencil_y_matrix(y_cells, 2 * y_cells))
    applied = pl.pallas_call(
        stencil_kernel,
        out_shape=jax.ShapeDtypeStruct(own.shape, jnp.bfloat16),
        in_specs=vmem(6),
        out_specs=vmem(1)[0],
        scratch_shapes=[pltpu.VMEM((planes, x_cells + 2 * RADIUS, bands, y_cells), jnp.float32)],
        compiler_params=pltpu.CompilerParams(vmem_limit_bytes=40 * 2**20),
        name="stencil",
    )(own, before, after, other, potential[:, :, None, :], matrix)

    partial_value = pl.pallas_call(
        lambda *refs: blocks_kernel(norm_scale, *refs),
        out_shape=jax.ShapeDtypeStruct((2, bands, bands), jnp.float32),
        in_specs=vmem(3),
        out_specs=vmem(1)[0],
        compiler_params=pltpu.CompilerParams(vmem_limit_bytes=40 * 2**20),
        name="blocks",
    )(own, applied, partner)

    mine = lax.dynamic_index_in_dim(partial_value, core, 0, keepdims=False)
    theirs = lax.dynamic_index_in_dim(partial_value, 1 - core, 0, keepdims=False)
    mine = mine + lax.ppermute(theirs, "ty", other_core)
    rows = bands // tx_count
    parts = lax.all_to_all(mine.reshape(tx_count, rows, bands), "tx", 0, 0)
    mine = jnp.sum(parts, 0)
    mirrored = lax.switch(plan_index, [back(plan) for plan in plan_list], mine)
    both = lax.all_gather(jnp.stack([mine, mirrored]), "tx")
    direct = both[:, 0].reshape(bands, bands)
    mirrored = both[:, 1].reshape(bands, bands).T
    low_first = (pair_masks[0] < pair_masks[1]).astype(jnp.int32)
    direct_first = later == low_first
    full = jnp.where(
        direct_first, jnp.stack([direct, mirrored]), jnp.stack([mirrored, direct])
    )
    full_other = lax.ppermute(full, "ty", other_core)
    gram = jnp.where(core == 0, full, full_other)
    ham = jnp.where(core == 0, full_other, full)
    return gram, ham


def solution(mesh):
    in_specs = (P("band", None, "tx", "ty"), P(None, "tx", "ty"), P())
    out_specs = (P(None, "band", None), P(None, "band", None))
    return jax.shard_map(body, mesh=mesh, in_specs=in_specs, out_specs=out_specs, check_vma=False)
```

```python
import jax
import jax.numpy as jnp
import numpy as np
from jax import lax
from jax.experimental import pallas as pl
from jax.experimental.pallas import tpu as pltpu
from jax.sharding import PartitionSpec as P

COEFFS = (
    -5369.0 / 1800.0,
    12.0 / 7.0,
    -15.0 / 56.0,
    10.0 / 189.0,
    -1.0 / 112.0,
    2.0 / 1925.0,
    -1.0 / 16632.0,
)
RADIUS = 6
GROUPS = 16
SIDES = 2
VMEM_LIMIT = 40 * 2**20


def receiving_side(mask, group):
    return 1 if group & (mask & -mask) else 0


def sends(mask):
    return [
        (group * SIDES + side, (group ^ mask) * SIDES + side)
        for group in range(GROUPS)
        for side in range(SIDES)
        if receiving_side(mask, group) != side
    ]


def by_mask(mask, value, pairs_of):
    branches = [
        lambda held, pairs=pairs_of(m): lax.ppermute(held, ("band", "ty"), pairs)
        for m in range(1, GROUPS)
    ]
    return lax.switch(mask - 1, branches, value)


def split(matrix):
    high = matrix.astype(jnp.bfloat16)
    low = (matrix - high.astype(np.float64)).astype(jnp.bfloat16)
    return np.concatenate([high, low], 1)


def along_matrix(cells):
    matrix = np.zeros((2 * cells, cells), np.float64)
    for cell in range(cells):
        for offset in range(1, RADIUS + 1):
            matrix[cell + offset, cell] += -0.5 * COEFFS[offset]
            if cell >= offset:
                matrix[cell - offset, cell] += -0.5 * COEFFS[offset]
    return split(matrix)


def before_matrix(cells):
    matrix = np.zeros((cells, cells), np.float64)
    for place in range(RADIUS):
        for cell in range(place + 1):
            matrix[cell, place] = -0.5 * COEFFS[RADIUS - place + cell]
    return split(matrix)


def pack_kernel(own_ref, other_ref, message_ref):
    planes, x_cells, bands, y_cells = own_ref.shape
    lane = lax.broadcasted_iota(jnp.int32, (bands, y_cells), 1)
    for z in range(planes):

        def step(x, packed, z=z):
            message_ref[z, x] = own_ref[z, x]
            edge = jnp.where(lane >= y_cells - RADIUS, other_ref[z, x].astype(jnp.float32), 0.0)
            return packed + pltpu.roll(edge, (x + 1) * RADIUS, 1)

        packed = lax.fori_loop(0, x_cells, step, jnp.zeros((bands, y_cells), jnp.float32))
        message_ref[z, x_cells] = packed.astype(jnp.bfloat16)


def stencil_kernel(
    own_ref, before_ref, after_ref, other_ref, potential_ref, along_ref, edge_ref, applied_ref, wide_ref
):
    planes, x_cells, bands, y_cells = other_ref.shape
    beta = COEFFS[1] + COEFFS[2] + COEFFS[4] + COEFFS[5]
    kappa = -0.5 * (3.0 * COEFFS[0] + 2.0 * COEFFS[3] + 2.0 * COEFFS[6] - beta)

    def widen(x, carry):
        for z in range(planes):
            wide_ref[z, RADIUS + x] = own_ref[z, x].astype(jnp.float32)
        return carry

    def widen_sides(x, carry):
        for z in range(planes):
            wide_ref[z, x] = before_ref[z, x].astype(jnp.float32)
            wide_ref[z, RADIUS + x_cells + x] = after_ref[z, x].astype(jnp.float32)
        return carry

    lax.fori_loop(0, x_cells, widen, 0)
    lax.fori_loop(0, RADIUS, widen_sides, 0)
    along = along_ref[...]
    edge = edge_ref[...]

    def step(x, packed):
        centers = [wide_ref[z, RADIUS + x] for z in range(planes)]
        plane_sum = (-0.5 * beta) * (centers[0] + centers[1] + centers[2])
        later = []
        for z in range(planes):
            own = own_ref[z, x]
            along_y = jnp.dot(
                jnp.concatenate([own, other_ref[z, x]], 1), along, preferred_element_type=jnp.float32
            )
            total = plane_sum + (potential_ref[z, x] + kappa) * centers[z]
            for offset in range(1, RADIUS + 1):
                total = total + (-0.5 * COEFFS[offset]) * (
                    wide_ref[z, RADIUS + x + offset] + wide_ref[z, RADIUS + x - offset]
                )
            total = total + (along_y[:, :y_cells] + along_y[:, y_cells:])
            applied_ref[z, x] = total.astype(jnp.bfloat16)
            outside = jnp.dot(own, edge, preferred_element_type=jnp.float32)
            outside = outside[:, :y_cells] + outside[:, y_cells:]
            later.append(packed[z] + pltpu.roll(outside, x * RADIUS, 1))
        return tuple(later)

    zero = jnp.zeros((bands, y_cells), jnp.float32)
    packed = lax.fori_loop(0, x_cells, step, (zero,) * planes)
    for z in range(planes):
        applied_ref[z, x_cells] = packed[z].astype(jnp.bfloat16)


def blocks_kernel(norm_scale, place_ref, own_ref, applied_ref, first_ref, second_ref, *out_refs):
    *part_refs, total_ref = out_refs
    planes, slabs, bands, _ = own_ref.shape
    rows = bands // len(part_refs)
    dims = (((1,), (1,)), ((), ()))
    for round_id, partner_ref in enumerate((first_ref, second_ref)):
        gram = jnp.zeros((bands, bands), jnp.float32)
        ham = jnp.zeros((bands, bands), jnp.float32)
        for z in range(planes):
            for x in range(0, slabs - 1, 2):
                pair = lambda ref: jnp.concatenate([ref[z, x], ref[z, x + 1]], 1)
                partner = pair(partner_ref)
                gram += lax.dot_general(pair(own_ref), partner, dims, preferred_element_type=jnp.float32)
                ham += lax.dot_general(pair(applied_ref), partner, dims, preferred_element_type=jnp.float32)
            ham += lax.dot_general(
                applied_ref[z, slabs - 1], partner_ref[z, slabs - 1], dims, preferred_element_type=jnp.float32
            )
        total_ref[2 * round_id] = gram * norm_scale
        total_ref[2 * round_id + 1] = ham * norm_scale
    count = len(part_refs)
    for step, part_ref in enumerate(part_refs):
        place = lax.rem(place_ref[0] + step, count)
        part_ref[...] = total_ref[:, pl.ds(pl.multiple_of(place * rows, rows), rows), :]


def gather_kernel(place_ref, *refs):
    *part_refs, out_ref = refs
    count = len(part_refs)
    rows = part_refs[0].shape[1]
    for step, part_ref in enumerate(part_refs):
        place = lax.rem(place_ref[0] - step + count, count)
        out_ref[:, pl.ds(pl.multiple_of(place * rows, rows), rows), :] = part_ref[...]


def finish_kernel(direct_ref, mine_ref, theirs_ref, gram_ref, ham_ref):
    for round_id in range(2):
        for kind, out_ref in enumerate((gram_ref, ham_ref)):
            mine = mine_ref[2 * round_id + kind]
            theirs = theirs_ref[2 * round_id + kind]
            is_direct = direct_ref[round_id] == 1
            direct = jnp.where(is_direct, mine, theirs)
            mirrored = jnp.where(is_direct, theirs, mine)
            out_ref[round_id] = direct + mirrored.T


def vmem(count):
    return [pl.BlockSpec(memory_space=pltpu.VMEM)] * count


def call(kernel, name, scalars, arrays, out_shapes, scratch=()):
    return pl.pallas_call(
        kernel,
        out_shape=out_shapes,
        in_specs=[pl.BlockSpec(memory_space=pltpu.SMEM)] * len(scalars) + vmem(len(arrays)),
        out_specs=vmem(1)[0] if not isinstance(out_shapes, list) else vmem(len(out_shapes)),
        scratch_shapes=list(scratch),
        compiler_params=pltpu.CompilerParams(vmem_limit_bytes=VMEM_LIMIT),
        name=name,
    )(*scalars, *arrays)


def body(orbitals, potential, pair_masks):
    bands, planes, x_cells, y_cells = orbitals.shape
    tx_count = lax.axis_size("tx")
    group = lax.axis_index("band")
    side = lax.axis_index("ty")
    place = lax.axis_index("tx").astype(jnp.int32)[None]
    norm_scale = float(planes * x_cells * y_cells * tx_count * SIDES) ** -0.5
    other_side = [(0, 1), (1, 0)]
    shifts = [[(i, (i + k) % tx_count) for i in range(tx_count)] for k in range(tx_count)]

    own = jnp.transpose(orbitals, (1, 2, 0, 3))
    other = lax.ppermute(own, "ty", other_side)
    before = lax.ppermute(own[:, x_cells - RADIUS :], "tx", shifts[1])
    after = lax.ppermute(own[:, :RADIUS], "tx", shifts[-1])
    slabs = jax.ShapeDtypeStruct((planes, x_cells + 1, bands, y_cells), jnp.bfloat16)
    message = call(pack_kernel, "pack", [], [own, other], slabs)
    partners = [by_mask(pair_masks[round_id], message, sends) for round_id in range(2)]

    applied = call(
        stencil_kernel,
        "stencil",
        [],
        [
            message,
            before,
            after,
            other,
            potential[:, :, None, :],
            jnp.asarray(along_matrix(y_cells)),
            jnp.asarray(before_matrix(y_cells)),
        ],
        slabs,
        [pltpu.VMEM((planes, x_cells + 2 * RADIUS, bands, y_cells), jnp.float32)],
    )
    part = jax.ShapeDtypeStruct((4, bands // tx_count, bands), jnp.float32)
    whole = jax.ShapeDtypeStruct((4, bands, bands), jnp.float32)
    parts = call(
        lambda *refs: blocks_kernel(norm_scale, *refs),
        "blocks",
        [place],
        [message, applied, *partners],
        [part] * tx_count,
        [pltpu.VMEM(whole.shape, whole.dtype)],
    )
    total = parts[0]
    for received in [lax.ppermute(parts[k], "tx", shifts[k]) for k in range(1, tx_count)]:
        total = total + received
    back = lambda mask: [(target, source) for source, target in sends(mask)]
    held = jnp.concatenate(
        [
            total[2 * round_id : 2 * round_id + 2]
            + by_mask(pair_masks[round_id], total[2 * round_id : 2 * round_id + 2], back)
            for round_id in range(2)
        ]
    )
    pieces = [held] + [lax.ppermute(held, "tx", shifts[k]) for k in range(1, tx_count)]
    mine = call(gather_kernel, "gather", [place], pieces, whole)
    theirs = lax.ppermute(mine, "ty", other_side)
    lowest = jnp.bitwise_and(pair_masks, -pair_masks)
    received_on = (jnp.bitwise_and(lowest, group) != 0).astype(jnp.int32)
    direct = (received_on == side).astype(jnp.int32)
    block = jax.ShapeDtypeStruct((2, bands, bands), jnp.float32)
    return call(finish_kernel, "finish", [direct], [mine, theirs], [block, block])


def solution(mesh):
    in_specs = (P("band", None, "tx", "ty"), P(None, "tx", "ty"), P())
    out_specs = (P(None, "band", None), P(None, "band", None))
    mapped = jax.shard_map(body, mesh=mesh, in_specs=in_specs, out_specs=out_specs, check_vma=False)
    return lambda *args: tuple(mapped(*args))
```

```python
import jax
import jax.numpy as jnp
import numpy as np
from jax import lax
from jax.experimental import pallas as pl
from jax.experimental.pallas import tpu as pltpu
from jax.sharding import PartitionSpec as P

COEFFS = (
    -5369.0 / 1800.0,
    12.0 / 7.0,
    -15.0 / 56.0,
    10.0 / 189.0,
    -1.0 / 112.0,
    2.0 / 1925.0,
    -1.0 / 16632.0,
)
RADIUS = 6
GROUPS = 16
SIDES = 2
VMEM_LIMIT = 40 * 2**20


def receiving_side(mask, group):
    return 1 if group & (mask & -mask) else 0


def sends(mask):
    return [
        (group * SIDES + side, (group ^ mask) * SIDES + side)
        for group in range(GROUPS)
        for side in range(SIDES)
        if receiving_side(mask, group) != side
    ]


def by_mask(mask, operands, pairs_of, beside=None):
    def branch(pairs):
        def run(value, *others):
            received = lax.ppermute(value, ("band", "ty"), pairs)
            return received if beside is None else (received, *beside(value, *others))

        return run

    return lax.switch(mask - 1, [branch(pairs_of(m)) for m in range(1, GROUPS)], *operands)


def split(matrix):
    high = matrix.astype(jnp.bfloat16)
    low = (matrix - high.astype(np.float64)).astype(jnp.bfloat16)
    return np.concatenate([high, low], 1)


def along_matrix(cells):
    matrix = np.zeros((2 * cells, cells), np.float64)
    for cell in range(cells):
        for offset in range(1, RADIUS + 1):
            matrix[cell + offset, cell] += -0.5 * COEFFS[offset]
            if cell >= offset:
                matrix[cell - offset, cell] += -0.5 * COEFFS[offset]
    return split(matrix)


def before_matrix(cells):
    matrix = np.zeros((cells, cells), np.float64)
    for place in range(RADIUS):
        for cell in range(place + 1):
            matrix[cell, place] = -0.5 * COEFFS[RADIUS - place + cell]
    return split(matrix)


def prepare_kernel(orbitals_ref, message_ref, head_ref, tail_ref, edges_ref):
    bands, planes, x_cells, y_cells = orbitals_ref.shape
    lane = lax.broadcasted_iota(jnp.int32, (bands, y_cells), 1)
    for z in range(planes):
        message_ref[z, :x_cells] = jnp.swapaxes(orbitals_ref[:, z], 0, 1)
        head_ref[z] = message_ref[z, :RADIUS]
        tail_ref[z] = message_ref[z, x_cells - RADIUS : x_cells]

        def step(x, packed, z=z):
            moved = pltpu.roll(message_ref[z, x].astype(jnp.float32), (x + 1) * RADIUS, 1)
            cell = lane - x * RADIUS
            last = jnp.where((cell >= 0) & (cell < RADIUS), moved, packed[0])
            first = jnp.where((cell >= RADIUS) & (cell < 2 * RADIUS), moved, packed[1])
            return last, first

        zero = jnp.zeros((bands, y_cells), jnp.float32)
        last, first = lax.fori_loop(0, x_cells, step, (zero, zero))
        edges_ref[0, z] = last.astype(jnp.bfloat16)
        edges_ref[1, z] = first.astype(jnp.bfloat16)
        message_ref[z, x_cells] = jnp.zeros((bands, y_cells), jnp.bfloat16)


def stencil(own_ref, before_ref, after_ref, edges_ref, potential_ref, along_ref, edge_ref, applied_ref, wide_ref):
    planes, slabs, bands, y_cells = own_ref.shape
    x_cells = slabs - 1
    beta = COEFFS[1] + COEFFS[2] + COEFFS[4] + COEFFS[5]
    kappa = -0.5 * (3.0 * COEFFS[0] + 2.0 * COEFFS[3] + 2.0 * COEFFS[6] - beta)

    def widen(x, carry):
        for z in range(planes):
            wide_ref[z, RADIUS + x] = own_ref[z, x].astype(jnp.float32)
        return carry

    def widen_sides(x, carry):
        for z in range(planes):
            wide_ref[z, x] = before_ref[z, x].astype(jnp.float32)
            wide_ref[z, RADIUS + x_cells + x] = after_ref[z, x].astype(jnp.float32)
        return carry

    lax.fori_loop(0, x_cells, widen, 0)
    lax.fori_loop(0, RADIUS, widen_sides, 0)
    along = along_ref[...]
    edge = edge_ref[...]

    def step(index, packed):
        z, x = index // x_cells, lax.rem(index, x_cells)
        own = own_ref[z, x]
        beside = pltpu.roll(edges_ref[1, z].astype(jnp.float32), y_cells - (x + 1) * RADIUS, 1)
        along_y = jnp.dot(
            jnp.concatenate([own, beside.astype(jnp.bfloat16)], 1), along, preferred_element_type=jnp.float32
        )
        row = RADIUS + x
        plane_sum = (-0.5 * beta) * (wide_ref[0, row] + wide_ref[1, row] + wide_ref[2, row])
        total = plane_sum + (potential_ref[z, x] + kappa) * wide_ref[z, row]
        for offset in range(1, RADIUS + 1):
            total = total + (-0.5 * COEFFS[offset]) * (wide_ref[z, row + offset] + wide_ref[z, row - offset])
        total = total + (along_y[:, :y_cells] + along_y[:, y_cells:])
        applied_ref[z, x] = total.astype(jnp.bfloat16)
        outside = jnp.dot(own, edge, preferred_element_type=jnp.float32)
        outside = outside[:, :y_cells] + outside[:, y_cells:]
        packed = jnp.where(x == 0, 0.0, packed) + pltpu.roll(outside, x * RADIUS, 1)

        @pl.when(x == x_cells - 1)
        def _():
            applied_ref[z, x_cells] = packed.astype(jnp.bfloat16)

        return packed

    lax.fori_loop(0, planes * x_cells, step, jnp.zeros((bands, y_cells), jnp.float32))


def pair_blocks(own_ref, applied_ref, partner_ref):
    planes, slabs, bands, _ = own_ref.shape
    dims = (((1,), (1,)), ((), ()))

    def plane(z, sums):
        gram, ham = sums
        for x in range(0, slabs - 1, 2):
            pair = lambda ref: jnp.concatenate([ref[z, x], ref[z, x + 1]], 1)
            partner = pair(partner_ref)
            gram += lax.dot_general(pair(own_ref), partner, dims, preferred_element_type=jnp.float32)
            ham += lax.dot_general(pair(applied_ref), partner, dims, preferred_element_type=jnp.float32)
        ham += lax.dot_general(
            applied_ref[z, slabs - 1], partner_ref[z, slabs - 1], dims, preferred_element_type=jnp.float32
        )
        return gram, ham

    zero = jnp.zeros((bands, bands), jnp.float32)
    return lax.fori_loop(0, planes, plane, (zero, zero))


def first_kernel(
    own_ref, before_ref, after_ref, edges_ref, potential_ref, along_ref, edge_ref, partner_ref,
    applied_ref, out_ref, wide_ref,
):
    stencil(
        own_ref, before_ref, after_ref, edges_ref, potential_ref, along_ref, edge_ref, applied_ref, wide_ref
    )
    out_ref[0], out_ref[1] = pair_blocks(own_ref, applied_ref, partner_ref)


def second_kernel(norm_scale, own_ref, applied_ref, partner_ref, before_ref, out_ref):
    places, _, rows, bands = out_ref.shape
    gram, ham = pair_blocks(own_ref, applied_ref, partner_ref)
    for index, block in enumerate((before_ref[0], before_ref[1], gram, ham)):
        out_ref[:, index] = (block * norm_scale).reshape(places, rows, bands)


def finish_kernel(direct_ref, mine_ref, theirs_ref, gram_ref, ham_ref):
    bands = mine_ref.shape[-1]
    for round_id in range(2):
        is_direct = direct_ref[round_id] == 1
        for kind, out_ref in enumerate((gram_ref, ham_ref)):
            mine = mine_ref[:, 2 * round_id + kind].reshape(bands, bands)
            theirs = theirs_ref[:, 2 * round_id + kind].reshape(bands, bands)
            direct = jnp.where(is_direct, mine, theirs)
            mirrored = jnp.where(is_direct, theirs, mine)
            out_ref[round_id] = direct + mirrored.T


def vmem(count):
    return [pl.BlockSpec(memory_space=pltpu.VMEM)] * count


def call(kernel, name, scalars, arrays, out_shapes, scratch=()):
    return pl.pallas_call(
        kernel,
        out_shape=out_shapes,
        in_specs=[pl.BlockSpec(memory_space=pltpu.SMEM)] * len(scalars) + vmem(len(arrays)),
        out_specs=vmem(1)[0] if not isinstance(out_shapes, list) else vmem(len(out_shapes)),
        scratch_shapes=list(scratch),
        compiler_params=pltpu.CompilerParams(vmem_limit_bytes=VMEM_LIMIT),
        name=name,
    )(*scalars, *arrays)


def body(orbitals, potential, pair_masks):
    bands, planes, x_cells, y_cells = orbitals.shape
    tx_count = lax.axis_size("tx")
    group = lax.axis_index("band")
    side = lax.axis_index("ty")
    norm_scale = float(planes * x_cells * y_cells * tx_count * SIDES) ** -0.5
    other_side = [(0, 1), (1, 0)]
    shape = lambda *sizes, dtype=jnp.float32: jax.ShapeDtypeStruct(sizes, dtype)

    slabs = shape(planes, x_cells + 1, bands, y_cells, dtype=jnp.bfloat16)
    rows = shape(planes, RADIUS, bands, y_cells, dtype=jnp.bfloat16)
    edges = shape(2, planes, bands, y_cells, dtype=jnp.bfloat16)
    message, head, tail, edges = call(prepare_kernel, "prepare", [], [orbitals], [slabs, rows, rows, edges])
    edges = lax.ppermute(edges, "ty", other_side)
    before = lax.ppermute(tail, "tx", [(i, (i + 1) % tx_count) for i in range(tx_count)])
    after = lax.ppermute(head, "tx", [((i + 1) % tx_count, i) for i in range(tx_count)])
    message = lax.dynamic_update_slice(message, edges[0][:, None], (0, x_cells, 0, 0))

    first = by_mask(pair_masks[0], [message], sends)
    beside = lambda own, *others: call(
        first_kernel,
        "first",
        [],
        [own, *others],
        [slabs, shape(2, bands, bands)],
        [pltpu.VMEM((planes, x_cells + 2 * RADIUS, bands, y_cells), jnp.float32)],
    )
    second, applied, first_blocks = by_mask(
        pair_masks[1],
        [
            message,
            before,
            after,
            edges,
            potential[:, :, None, :],
            jnp.asarray(along_matrix(y_cells)),
            jnp.asarray(before_matrix(y_cells)),
            first,
        ],
        sends,
        beside,
    )
    partial_value = call(
        lambda *refs: second_kernel(norm_scale, *refs),
        "second",
        [],
        [message, applied, second, first_blocks],
        shape(tx_count, 4, bands // tx_count, bands),
    )
    total = jnp.sum(lax.all_to_all(partial_value, "tx", 0, 0), 0)
    back = lambda mask: [(target, source) for source, target in sends(mask)]
    held = jnp.concatenate(
        [
            total[2 * round_id : 2 * round_id + 2]
            + by_mask(pair_masks[round_id], [total[2 * round_id : 2 * round_id + 2]], back)
            for round_id in range(2)
        ]
    )
    mine = lax.all_to_all(jnp.broadcast_to(held, (tx_count, *held.shape)), "tx", 0, 0)
    theirs = lax.ppermute(mine, "ty", other_side)
    lowest = jnp.bitwise_and(pair_masks, -pair_masks)
    received_on = (jnp.bitwise_and(lowest, group) != 0).astype(jnp.int32)
    direct = (received_on == side).astype(jnp.int32)
    block = shape(2, bands, bands)
    return call(finish_kernel, "finish", [direct], [mine, theirs], [block, block])


def solution(mesh):
    in_specs = (P("band", None, "tx", "ty"), P(None, "tx", "ty"), P())
    out_specs = (P(None, "band", None), P(None, "band", None))
    mapped = jax.shard_map(body, mesh=mesh, in_specs=in_specs, out_specs=out_specs, check_vma=False)
    return lambda *args: tuple(mapped(*args))
```

```python
import jax
import jax.numpy as jnp
import numpy as np
from jax import lax
from jax.experimental import pallas as pl
from jax.experimental.pallas import tpu as pltpu
from jax.sharding import PartitionSpec as P

COEFFS = (
    -5369.0 / 1800.0,
    12.0 / 7.0,
    -15.0 / 56.0,
    10.0 / 189.0,
    -1.0 / 112.0,
    2.0 / 1925.0,
    -1.0 / 16632.0,
)
RADIUS = 6
GROUPS = 16
SIDES = 2
VMEM_LIMIT = 40 * 2**20


def receiving_side(mask, group):
    return 1 if group & (mask & -mask) else 0


def sends(mask):
    return [
        (group * SIDES + side, (group ^ mask) * SIDES + side)
        for group in range(GROUPS)
        for side in range(SIDES)
        if receiving_side(mask, group) != side
    ]


def by_mask(mask, operands, pairs_of, beside=None):
    def branch(pairs):
        def run(value, *others):
            received = lax.ppermute(value, ("band", "ty"), pairs)
            return received if beside is None else (received, *beside(value, *others))

        return run

    return lax.switch(mask - 1, [branch(pairs_of(m)) for m in range(1, GROUPS)], *operands)


def split(matrix):
    high = matrix.astype(jnp.bfloat16)
    low = (matrix - high.astype(np.float64)).astype(jnp.bfloat16)
    return np.concatenate([high, low], 1)


def along_matrix(cells):
    matrix = np.zeros((2 * cells, cells), np.float64)
    for cell in range(cells):
        for offset in range(1, RADIUS + 1):
            matrix[cell + offset, cell] += -0.5 * COEFFS[offset]
            if cell >= offset:
                matrix[cell - offset, cell] += -0.5 * COEFFS[offset]
    return split(matrix)


def before_matrix(cells):
    matrix = np.zeros((cells, cells), np.float64)
    for place in range(RADIUS):
        for cell in range(place + 1):
            matrix[cell, place] = -0.5 * COEFFS[RADIUS - place + cell]
    return split(matrix)


def prepare_kernel(orbitals_ref, message_ref, head_ref, tail_ref, edges_ref):
    bands, _, x_cells, y_cells = orbitals_ref.shape
    lane = lax.broadcasted_iota(jnp.int32, (bands, y_cells), 1)
    message_ref[0, :x_cells] = jnp.swapaxes(orbitals_ref[:, 0], 0, 1)
    head_ref[0] = message_ref[0, :RADIUS]
    tail_ref[0] = message_ref[0, x_cells - RADIUS : x_cells]
    last = jnp.zeros((bands, y_cells), jnp.float32)
    first = last
    for x in range(x_cells):
        moved = pltpu.roll(message_ref[0, x].astype(jnp.float32), (x + 1) * RADIUS, 1)
        cell = lane - x * RADIUS
        last = jnp.where((cell >= 0) & (cell < RADIUS), moved, last)
        first = jnp.where((cell >= RADIUS) & (cell < 2 * RADIUS), moved, first)
    edges_ref[0, 0] = last.astype(jnp.bfloat16)
    edges_ref[1, 0] = first.astype(jnp.bfloat16)
    message_ref[0, x_cells] = jnp.zeros((bands, y_cells), jnp.bfloat16)


def prepare(orbitals):
    bands, planes, x_cells, y_cells = orbitals.shape
    plane = lambda *lead: pl.BlockSpec((1, *lead, bands, y_cells), lambda z: (z, *[0] * (len(lead) + 2)))
    array = lambda *lead: jax.ShapeDtypeStruct((*lead, bands, y_cells), jnp.bfloat16)
    return pl.pallas_call(
        prepare_kernel,
        grid=(planes,),
        in_specs=[pl.BlockSpec((bands, 1, x_cells, y_cells), lambda z: (0, z, 0, 0))],
        out_specs=[
            plane(x_cells + 1),
            plane(RADIUS),
            plane(RADIUS),
            pl.BlockSpec((2, 1, bands, y_cells), lambda z: (0, z, 0, 0)),
        ],
        out_shape=[array(planes, x_cells + 1), array(planes, RADIUS), array(planes, RADIUS), array(2, planes)],
        compiler_params=pltpu.CompilerParams(vmem_limit_bytes=VMEM_LIMIT),
        name="prepare",
    )(orbitals)


def stencil(own_ref, before_ref, after_ref, edges_ref, potential_ref, along_ref, edge_ref, applied_ref, wide_ref):
    planes, slabs, bands, y_cells = own_ref.shape
    x_cells = slabs - 1
    beta = COEFFS[1] + COEFFS[2] + COEFFS[4] + COEFFS[5]
    kappa = -0.5 * (3.0 * COEFFS[0] + 2.0 * COEFFS[3] + 2.0 * COEFFS[6] - beta)

    def widen(x, carry):
        for z in range(planes):
            wide_ref[z, RADIUS + x] = own_ref[z, x].astype(jnp.float32)
        return carry

    def widen_sides(x, carry):
        for z in range(planes):
            wide_ref[z, x] = before_ref[z, x].astype(jnp.float32)
            wide_ref[z, RADIUS + x_cells + x] = after_ref[z, x].astype(jnp.float32)
        return carry

    lax.fori_loop(0, x_cells, widen, 0)
    lax.fori_loop(0, RADIUS, widen_sides, 0)
    along = along_ref[...]
    edge = edge_ref[...]

    def step(x, packed):
        row = RADIUS + x
        centers = [wide_ref[z, row] for z in range(planes)]
        plane_sum = (-0.5 * beta) * sum(centers)
        later = []
        for z in range(planes):
            own = own_ref[z, x]
            beside = pltpu.roll(edges_ref[1, z].astype(jnp.float32), y_cells - (x + 1) * RADIUS, 1)
            along_y = jnp.dot(
                jnp.concatenate([own, beside.astype(jnp.bfloat16)], 1), along, preferred_element_type=jnp.float32
            )
            total = plane_sum + (potential_ref[z, x] + kappa) * centers[z]
            for offset in range(1, RADIUS + 1):
                total = total + (-0.5 * COEFFS[offset]) * (wide_ref[z, row + offset] + wide_ref[z, row - offset])
            total = total + (along_y[:, :y_cells] + along_y[:, y_cells:])
            applied_ref[z, x] = total.astype(jnp.bfloat16)
            outside = jnp.dot(own, edge, preferred_element_type=jnp.float32)
            outside = outside[:, :y_cells] + outside[:, y_cells:]
            later.append(packed[z] + pltpu.roll(outside, x * RADIUS, 1))
        return tuple(later)

    zero = jnp.zeros((bands, y_cells), jnp.float32)
    packed = lax.fori_loop(0, x_cells, step, (zero,) * planes)
    for z in range(planes):
        applied_ref[z, x_cells] = packed[z].astype(jnp.bfloat16)


def pair_blocks(own_ref, applied_ref, partner_ref):
    planes, slabs, bands, _ = own_ref.shape
    dims = (((1,), (1,)), ((), ()))

    def plane(z, sums):
        gram, ham = sums
        for x in range(0, slabs - 1, 2):
            pair = lambda ref: jnp.concatenate([ref[z, x], ref[z, x + 1]], 1)
            partner = pair(partner_ref)
            gram += lax.dot_general(pair(own_ref), partner, dims, preferred_element_type=jnp.float32)
            ham += lax.dot_general(pair(applied_ref), partner, dims, preferred_element_type=jnp.float32)
        ham += lax.dot_general(
            applied_ref[z, slabs - 1], partner_ref[z, slabs - 1], dims, preferred_element_type=jnp.float32
        )
        return gram, ham

    zero = jnp.zeros((bands, bands), jnp.float32)
    return lax.fori_loop(0, planes, plane, (zero, zero))


def first_kernel(
    own_ref, before_ref, after_ref, edges_ref, potential_ref, along_ref, edge_ref, partner_ref,
    applied_ref, out_ref, wide_ref,
):
    stencil(
        own_ref, before_ref, after_ref, edges_ref, potential_ref, along_ref, edge_ref, applied_ref, wide_ref
    )
    out_ref[0], out_ref[1] = pair_blocks(own_ref, applied_ref, partner_ref)


def second_kernel(norm_scale, own_ref, applied_ref, partner_ref, before_ref, out_ref):
    places, _, rows, bands = out_ref.shape
    gram, ham = pair_blocks(own_ref, applied_ref, partner_ref)
    for index, block in enumerate((before_ref[0], before_ref[1], gram, ham)):
        out_ref[:, index] = (block * norm_scale).reshape(places, rows, bands)


def finish_kernel(direct_ref, mine_ref, theirs_ref, gram_ref, ham_ref):
    bands = mine_ref.shape[-1]
    for round_id in range(2):
        is_direct = direct_ref[round_id] == 1
        for kind, out_ref in enumerate((gram_ref, ham_ref)):
            mine = mine_ref[:, 2 * round_id + kind].reshape(bands, bands)
            theirs = theirs_ref[:, 2 * round_id + kind].reshape(bands, bands)
            direct = jnp.where(is_direct, mine, theirs)
            mirrored = jnp.where(is_direct, theirs, mine)
            out_ref[round_id] = direct + mirrored.T


def vmem(count):
    return [pl.BlockSpec(memory_space=pltpu.VMEM)] * count


def call(kernel, name, scalars, arrays, out_shapes, scratch=()):
    return pl.pallas_call(
        kernel,
        out_shape=out_shapes,
        in_specs=[pl.BlockSpec(memory_space=pltpu.SMEM)] * len(scalars) + vmem(len(arrays)),
        out_specs=vmem(1)[0] if not isinstance(out_shapes, list) else vmem(len(out_shapes)),
        scratch_shapes=list(scratch),
        compiler_params=pltpu.CompilerParams(vmem_limit_bytes=VMEM_LIMIT),
        name=name,
    )(*scalars, *arrays)


def body(orbitals, potential, pair_masks):
    bands, planes, x_cells, y_cells = orbitals.shape
    tx_count = lax.axis_size("tx")
    group = lax.axis_index("band")
    side = lax.axis_index("ty")
    norm_scale = float(planes * x_cells * y_cells * tx_count * SIDES) ** -0.5
    other_side = [(0, 1), (1, 0)]
    shape = lambda *sizes, dtype=jnp.float32: jax.ShapeDtypeStruct(sizes, dtype)

    slabs = shape(planes, x_cells + 1, bands, y_cells, dtype=jnp.bfloat16)
    message, head, tail, edges = prepare(orbitals)
    edges = lax.ppermute(edges, "ty", other_side)
    message = lax.dynamic_update_slice(message, edges[0][:, None], (0, x_cells, 0, 0))
    message, head, tail = lax.optimization_barrier((message, head, tail))
    before = lax.ppermute(tail, "tx", [(i, (i + 1) % tx_count) for i in range(tx_count)])
    after = lax.ppermute(head, "tx", [((i + 1) % tx_count, i) for i in range(tx_count)])

    first = by_mask(pair_masks[0], [message], sends)
    beside = lambda own, *others: call(
        first_kernel,
        "first",
        [],
        [own, *others],
        [slabs, shape(2, bands, bands)],
        [pltpu.VMEM((planes, x_cells + 2 * RADIUS, bands, y_cells), jnp.float32)],
    )
    second, applied, first_blocks = by_mask(
        pair_masks[1],
        [
            message,
            before,
            after,
            edges,
            potential[:, :, None, :],
            jnp.asarray(along_matrix(y_cells)),
            jnp.asarray(before_matrix(y_cells)),
            first,
        ],
        sends,
        beside,
    )
    partial_value = call(
        lambda *refs: second_kernel(norm_scale, *refs),
        "second",
        [],
        [message, applied, second, first_blocks],
        shape(tx_count, 4, bands // tx_count, bands),
    )
    total = jnp.sum(lax.all_to_all(partial_value, "tx", 0, 0), 0)
    back = lambda mask: [(target, source) for source, target in sends(mask)]
    held = jnp.concatenate(
        [
            total[2 * round_id : 2 * round_id + 2]
            + by_mask(pair_masks[round_id], [total[2 * round_id : 2 * round_id + 2]], back)
            for round_id in range(2)
        ]
    )
    mine = lax.all_to_all(jnp.broadcast_to(held, (tx_count, *held.shape)), "tx", 0, 0)
    theirs = lax.ppermute(mine, "ty", other_side)
    lowest = jnp.bitwise_and(pair_masks, -pair_masks)
    received_on = (jnp.bitwise_and(lowest, group) != 0).astype(jnp.int32)
    direct = (received_on == side).astype(jnp.int32)
    block = shape(2, bands, bands)
    return call(finish_kernel, "finish", [direct], [mine, theirs], [block, block])


def solution(mesh):
    in_specs = (P("band", None, "tx", "ty"), P(None, "tx", "ty"), P())
    out_specs = (P(None, "band", None), P(None, "band", None))
    mapped = jax.shard_map(body, mesh=mesh, in_specs=in_specs, out_specs=out_specs, check_vma=False)
    return lambda *args: tuple(mapped(*args))
```

```python
import jax
import jax.numpy as jnp
import numpy as np
from jax import lax
from jax.experimental import pallas as pl
from jax.experimental.pallas import tpu as pltpu
from jax.sharding import PartitionSpec as P

COEFFS = (
    -5369.0 / 1800.0,
    12.0 / 7.0,
    -15.0 / 56.0,
    10.0 / 189.0,
    -1.0 / 112.0,
    2.0 / 1925.0,
    -1.0 / 16632.0,
)
RADIUS = 6
GROUPS = 16
SIDES = 2
VMEM_LIMIT = 40 * 2**20


def receiving_side(mask, group):
    return 1 if group & (mask & -mask) else 0


def sends(mask):
    return [
        (group * SIDES + side, (group ^ mask) * SIDES + side)
        for group in range(GROUPS)
        for side in range(SIDES)
        if receiving_side(mask, group) != side
    ]


def by_mask(index, operands, pairs_of, beside=None):
    def branch(pairs):
        def run(value, *others):
            received = lax.ppermute(value, ("band", "ty"), pairs)
            return received if beside is None else (received, *beside(value, *others))

        return run

    return lax.switch(index, [branch(pairs_of(m)) for m in range(1, GROUPS)], *operands)


def split(matrix):
    high = matrix.astype(jnp.bfloat16)
    low = (matrix - high.astype(np.float64)).astype(jnp.bfloat16)
    return np.concatenate([high, low], 1)


def along_matrix(cells):
    matrix = np.zeros((2 * cells, cells), np.float64)
    for cell in range(cells):
        for offset in range(1, RADIUS + 1):
            matrix[cell + offset, cell] += -0.5 * COEFFS[offset]
            if cell >= offset:
                matrix[cell - offset, cell] += -0.5 * COEFFS[offset]
    return split(matrix)


def before_matrix(cells):
    matrix = np.zeros((cells, cells), np.float64)
    for place in range(RADIUS):
        for cell in range(place + 1):
            matrix[cell, place] = -0.5 * COEFFS[RADIUS - place + cell]
    return split(matrix)


def prepare_kernel(orbitals_ref, message_ref, head_ref, tail_ref, edges_ref):
    bands, _, x_cells, y_cells = orbitals_ref.shape
    lane = lax.broadcasted_iota(jnp.int32, (bands, y_cells), 1)
    message_ref[0, :x_cells] = jnp.swapaxes(orbitals_ref[:, 0], 0, 1)
    head_ref[0] = message_ref[0, :RADIUS]
    tail_ref[0] = message_ref[0, x_cells - RADIUS : x_cells]
    last = jnp.zeros((bands, y_cells), jnp.float32)
    first = last
    for x in range(x_cells):
        moved = pltpu.roll(message_ref[0, x].astype(jnp.float32), (x + 1) * RADIUS, 1)
        cell = lane - x * RADIUS
        last = jnp.where((cell >= 0) & (cell < RADIUS), moved, last)
        first = jnp.where((cell >= RADIUS) & (cell < 2 * RADIUS), moved, first)
    edges_ref[0, 0] = last.astype(jnp.bfloat16)
    edges_ref[1, 0] = first.astype(jnp.bfloat16)
    message_ref[0, x_cells] = jnp.zeros((bands, y_cells), jnp.bfloat16)


def prepare(orbitals):
    bands, planes, x_cells, y_cells = orbitals.shape
    plane = lambda *lead: pl.BlockSpec((1, *lead, bands, y_cells), lambda z: (z, *[0] * (len(lead) + 2)))
    array = lambda *lead: jax.ShapeDtypeStruct((*lead, bands, y_cells), jnp.bfloat16)
    return pl.pallas_call(
        prepare_kernel,
        grid=(planes,),
        in_specs=[pl.BlockSpec((bands, 1, x_cells, y_cells), lambda z: (0, z, 0, 0))],
        out_specs=[
            plane(x_cells + 1),
            plane(RADIUS),
            plane(RADIUS),
            pl.BlockSpec((2, 1, bands, y_cells), lambda z: (0, z, 0, 0)),
        ],
        out_shape=[array(planes, x_cells + 1), array(planes, RADIUS), array(planes, RADIUS), array(2, planes)],
        compiler_params=pltpu.CompilerParams(vmem_limit_bytes=VMEM_LIMIT),
        name="prepare",
    )(orbitals)


def stencil(own_ref, before_ref, after_ref, edges_ref, potential_ref, along_ref, edge_ref, applied_ref, wide_ref):
    planes, slabs, bands, y_cells = own_ref.shape
    x_cells = slabs - 1
    beta = COEFFS[1] + COEFFS[2] + COEFFS[4] + COEFFS[5]
    kappa = -0.5 * (3.0 * COEFFS[0] + 2.0 * COEFFS[3] + 2.0 * COEFFS[6] - beta)

    def widen(x, carry):
        for z in range(planes):
            wide_ref[z, RADIUS + x] = own_ref[z, x].astype(jnp.float32)
        return carry

    def widen_sides(x, carry):
        for z in range(planes):
            wide_ref[z, x] = before_ref[z, x].astype(jnp.float32)
            wide_ref[z, RADIUS + x_cells + x] = after_ref[z, x].astype(jnp.float32)
        return carry

    lax.fori_loop(0, x_cells, widen, 0)
    lax.fori_loop(0, RADIUS, widen_sides, 0)
    along = along_ref[...]
    edge = edge_ref[...]

    def step(x, packed):
        row = RADIUS + x
        centers = [wide_ref[z, row] for z in range(planes)]
        plane_sum = (-0.5 * beta) * sum(centers)
        later = []
        for z in range(planes):
            own = own_ref[z, x]
            beside = pltpu.roll(edges_ref[1, z].astype(jnp.float32), y_cells - (x + 1) * RADIUS, 1)
            along_y = jnp.dot(
                jnp.concatenate([own, beside.astype(jnp.bfloat16)], 1), along, preferred_element_type=jnp.float32
            )
            total = plane_sum + (potential_ref[z, x] + kappa) * centers[z]
            for offset in range(1, RADIUS + 1):
                total = total + (-0.5 * COEFFS[offset]) * (wide_ref[z, row + offset] + wide_ref[z, row - offset])
            total = total + (along_y[:, :y_cells] + along_y[:, y_cells:])
            applied_ref[z, x] = total.astype(jnp.bfloat16)
            outside = jnp.dot(own, edge, preferred_element_type=jnp.float32)
            outside = outside[:, :y_cells] + outside[:, y_cells:]
            later.append(packed[z] + pltpu.roll(outside, x * RADIUS, 1))
        return tuple(later)

    zero = jnp.zeros((bands, y_cells), jnp.float32)
    packed = lax.fori_loop(0, x_cells, step, (zero,) * planes)
    for z in range(planes):
        applied_ref[z, x_cells] = packed[z].astype(jnp.bfloat16)


def pair_blocks(own_ref, applied_ref, partner_ref):
    planes, slabs, bands, _ = own_ref.shape
    dims = (((1,), (1,)), ((), ()))

    def plane(z, sums):
        gram, ham = sums
        for x in range(0, slabs - 1, 2):
            pair = lambda ref: jnp.concatenate([ref[z, x], ref[z, x + 1]], 1)
            partner = pair(partner_ref)
            gram += lax.dot_general(pair(own_ref), partner, dims, preferred_element_type=jnp.float32)
            ham += lax.dot_general(pair(applied_ref), partner, dims, preferred_element_type=jnp.float32)
        ham += lax.dot_general(
            applied_ref[z, slabs - 1], partner_ref[z, slabs - 1], dims, preferred_element_type=jnp.float32
        )
        return gram, ham

    zero = jnp.zeros((bands, bands), jnp.float32)
    return lax.fori_loop(0, planes, plane, (zero, zero))


def first_kernel(
    own_ref, before_ref, after_ref, edges_ref, potential_ref, along_ref, edge_ref, partner_ref,
    applied_ref, out_ref, wide_ref,
):
    stencil(
        own_ref, before_ref, after_ref, edges_ref, potential_ref, along_ref, edge_ref, applied_ref, wide_ref
    )
    out_ref[0], out_ref[1] = pair_blocks(own_ref, applied_ref, partner_ref)


def second_kernel(norm_scale, own_ref, applied_ref, partner_ref, before_ref, out_ref):
    places, _, rows, bands = out_ref.shape
    gram, ham = pair_blocks(own_ref, applied_ref, partner_ref)
    for index, block in enumerate((before_ref[0], before_ref[1], gram, ham)):
        out_ref[:, index] = (block * norm_scale).reshape(places, rows, bands)


def finish_kernel(direct_ref, mine_ref, theirs_ref, gram_ref, ham_ref):
    bands = mine_ref.shape[-1]
    for round_id in range(2):
        is_direct = direct_ref[round_id] == 1
        for kind, out_ref in enumerate((gram_ref, ham_ref)):
            mine = mine_ref[:, 2 * round_id + kind].reshape(bands, bands)
            theirs = theirs_ref[:, 2 * round_id + kind].reshape(bands, bands)
            direct = jnp.where(is_direct, mine, theirs)
            mirrored = jnp.where(is_direct, theirs, mine)
            out_ref[round_id] = direct + mirrored.T


def vmem(count):
    return [pl.BlockSpec(memory_space=pltpu.VMEM)] * count


def call(kernel, name, scalars, arrays, out_shapes, scratch=()):
    return pl.pallas_call(
        kernel,
        out_shape=out_shapes,
        in_specs=[pl.BlockSpec(memory_space=pltpu.SMEM)] * len(scalars) + vmem(len(arrays)),
        out_specs=vmem(1)[0] if not isinstance(out_shapes, list) else vmem(len(out_shapes)),
        scratch_shapes=list(scratch),
        compiler_params=pltpu.CompilerParams(vmem_limit_bytes=VMEM_LIMIT),
        name=name,
    )(*scalars, *arrays)


def body(orbitals, potential, pair_masks):
    bands, planes, x_cells, y_cells = orbitals.shape
    tx_count = lax.axis_size("tx")
    group = lax.axis_index("band")
    side = lax.axis_index("ty")
    norm_scale = float(planes * x_cells * y_cells * tx_count * SIDES) ** -0.5
    other_side = [(0, 1), (1, 0)]
    shape = lambda *sizes, dtype=jnp.float32: jax.ShapeDtypeStruct(sizes, dtype)

    slabs = shape(planes, x_cells + 1, bands, y_cells, dtype=jnp.bfloat16)
    message, head, tail, edges = prepare(orbitals)
    edges = lax.ppermute(edges, "ty", other_side)
    masks = [pair_masks[0] - 1, pair_masks[1] - 1]
    message, *masks = lax.optimization_barrier((message, *masks))
    message = lax.dynamic_update_slice(message, edges[0][:, None], (0, x_cells, 0, 0))
    before = lax.ppermute(tail, "tx", [(i, (i + 1) % tx_count) for i in range(tx_count)])
    after = lax.ppermute(head, "tx", [((i + 1) % tx_count, i) for i in range(tx_count)])

    first = by_mask(masks[0], [message], sends)
    beside = lambda own, *others: call(
        first_kernel,
        "first",
        [],
        [own, *others],
        [slabs, shape(2, bands, bands)],
        [pltpu.VMEM((planes, x_cells + 2 * RADIUS, bands, y_cells), jnp.float32)],
    )
    second, applied, first_blocks = by_mask(
        masks[1],
        [
            message,
            before,
            after,
            edges,
            potential[:, :, None, :],
            jnp.asarray(along_matrix(y_cells)),
            jnp.asarray(before_matrix(y_cells)),
            first,
        ],
        sends,
        beside,
    )
    partial_value = call(
        lambda *refs: second_kernel(norm_scale, *refs),
        "second",
        [],
        [message, applied, second, first_blocks],
        shape(tx_count, 4, bands // tx_count, bands),
    )
    total = jnp.sum(lax.all_to_all(partial_value, "tx", 0, 0), 0)
    back = lambda mask: [(target, source) for source, target in sends(mask)]
    held = jnp.concatenate(
        [
            total[2 * round_id : 2 * round_id + 2]
            + by_mask(masks[round_id], [total[2 * round_id : 2 * round_id + 2]], back)
            for round_id in range(2)
        ]
    )
    mine = lax.all_to_all(jnp.broadcast_to(held, (tx_count, *held.shape)), "tx", 0, 0)
    theirs = lax.ppermute(mine, "ty", other_side)
    lowest = jnp.bitwise_and(pair_masks, -pair_masks)
    received_on = (jnp.bitwise_and(lowest, group) != 0).astype(jnp.int32)
    direct = (received_on == side).astype(jnp.int32)
    block = shape(2, bands, bands)
    return call(finish_kernel, "finish", [direct], [mine, theirs], [block, block])


def solution(mesh):
    in_specs = (P("band", None, "tx", "ty"), P(None, "tx", "ty"), P())
    out_specs = (P(None, "band", None), P(None, "band", None))
    mapped = jax.shard_map(body, mesh=mesh, in_specs=in_specs, out_specs=out_specs, check_vma=False)
    return lambda *args: tuple(mapped(*args))
```

```python
import jax
import jax.numpy as jnp
import numpy as np
from jax import lax
from jax.experimental import pallas as pl
from jax.experimental.pallas import tpu as pltpu
from jax.sharding import PartitionSpec as P

COEFFS = (
    -5369.0 / 1800.0,
    12.0 / 7.0,
    -15.0 / 56.0,
    10.0 / 189.0,
    -1.0 / 112.0,
    2.0 / 1925.0,
    -1.0 / 16632.0,
)
RADIUS = 6
GROUPS = 16
SIDES = 2
VMEM_LIMIT = 40 * 2**20


def receiving_side(mask, group):
    return 1 if group & (mask & -mask) else 0


def sends(mask):
    return [
        (group * SIDES + side, (group ^ mask) * SIDES + side)
        for group in range(GROUPS)
        for side in range(SIDES)
        if receiving_side(mask, group) != side
    ]


def relays(change):
    return [
        (group * SIDES + (group & 1), (group ^ change) * SIDES + (group & 1)) for group in range(GROUPS)
    ]


RELAYED = (4, 8)


def first_by_mask(index, value, next_index):
    def branch(mask):
        def run(held, following):
            received = lax.ppermute(held, ("band", "ty"), sends(mask))
            chosen = following
            if mask & 1:
                for place, change in enumerate(RELAYED):
                    chosen = jnp.where(following == (mask ^ change) - 1, GROUPS - 1 + place, chosen)
            return received, chosen

        return run

    return lax.switch(index, [branch(mask) for mask in range(1, GROUPS)], value, next_index)


def second_by_mask(index, operands, beside):
    def branch(pairs, which):
        def run(*held):
            return lax.ppermute(held[which], ("band", "ty"), pairs), *beside(*held)

        return run

    branches = [branch(sends(mask), 0) for mask in range(1, GROUPS)]
    branches += [branch(relays(change), -1) for change in RELAYED]
    return lax.switch(index, branches, *operands)


def back_by_mask(index, value):
    back = lambda mask: [(target, source) for source, target in sends(mask)]
    branch = lambda pairs: lambda held: lax.ppermute(held, ("band", "ty"), pairs)
    return lax.switch(index, [branch(back(mask)) for mask in range(1, GROUPS)], value)


def split(matrix):
    high = matrix.astype(jnp.bfloat16)
    low = (matrix - high.astype(np.float64)).astype(jnp.bfloat16)
    return np.concatenate([high, low], 1)


def along_matrix(cells):
    matrix = np.zeros((2 * cells, cells), np.float64)
    for cell in range(cells):
        for offset in range(1, RADIUS + 1):
            matrix[cell + offset, cell] += -0.5 * COEFFS[offset]
            if cell >= offset:
                matrix[cell - offset, cell] += -0.5 * COEFFS[offset]
    return split(matrix)


def before_matrix(cells):
    matrix = np.zeros((cells, cells), np.float64)
    for place in range(RADIUS):
        for cell in range(place + 1):
            matrix[cell, place] = -0.5 * COEFFS[RADIUS - place + cell]
    return split(matrix)


def prepare_kernel(orbitals_ref, message_ref, head_ref, tail_ref, edges_ref):
    bands, _, x_cells, y_cells = orbitals_ref.shape
    lane = lax.broadcasted_iota(jnp.int32, (bands, y_cells), 1)
    message_ref[0, :x_cells] = jnp.swapaxes(orbitals_ref[:, 0], 0, 1)
    head_ref[0] = message_ref[0, :RADIUS]
    tail_ref[0] = message_ref[0, x_cells - RADIUS : x_cells]
    last = jnp.zeros((bands, y_cells), jnp.float32)
    first = last
    for x in range(x_cells):
        moved = pltpu.roll(message_ref[0, x].astype(jnp.float32), (x + 1) * RADIUS, 1)
        cell = lane - x * RADIUS
        last = jnp.where((cell >= 0) & (cell < RADIUS), moved, last)
        first = jnp.where((cell >= RADIUS) & (cell < 2 * RADIUS), moved, first)
    edges_ref[0, 0] = last.astype(jnp.bfloat16)
    edges_ref[1, 0] = first.astype(jnp.bfloat16)
    message_ref[0, x_cells] = jnp.zeros((bands, y_cells), jnp.bfloat16)


def prepare(orbitals):
    bands, planes, x_cells, y_cells = orbitals.shape
    plane = lambda *lead: pl.BlockSpec((1, *lead, bands, y_cells), lambda z: (z, *[0] * (len(lead) + 2)))
    array = lambda *lead: jax.ShapeDtypeStruct((*lead, bands, y_cells), jnp.bfloat16)
    return pl.pallas_call(
        prepare_kernel,
        grid=(planes,),
        in_specs=[pl.BlockSpec((bands, 1, x_cells, y_cells), lambda z: (0, z, 0, 0))],
        out_specs=[
            plane(x_cells + 1),
            plane(RADIUS),
            plane(RADIUS),
            pl.BlockSpec((2, 1, bands, y_cells), lambda z: (0, z, 0, 0)),
        ],
        out_shape=[array(planes, x_cells + 1), array(planes, RADIUS), array(planes, RADIUS), array(2, planes)],
        compiler_params=pltpu.CompilerParams(vmem_limit_bytes=VMEM_LIMIT),
        name="prepare",
    )(orbitals)


def stencil(own_ref, before_ref, after_ref, edges_ref, potential_ref, along_ref, edge_ref, applied_ref, wide_ref):
    planes, slabs, bands, y_cells = own_ref.shape
    x_cells = slabs - 1
    beta = COEFFS[1] + COEFFS[2] + COEFFS[4] + COEFFS[5]
    kappa = -0.5 * (3.0 * COEFFS[0] + 2.0 * COEFFS[3] + 2.0 * COEFFS[6] - beta)

    def widen(x, carry):
        for z in range(planes):
            wide_ref[z, RADIUS + x] = own_ref[z, x].astype(jnp.float32)
        return carry

    def widen_sides(x, carry):
        for z in range(planes):
            wide_ref[z, x] = before_ref[z, x].astype(jnp.float32)
            wide_ref[z, RADIUS + x_cells + x] = after_ref[z, x].astype(jnp.float32)
        return carry

    lax.fori_loop(0, x_cells, widen, 0)
    lax.fori_loop(0, RADIUS, widen_sides, 0)
    along = along_ref[...]
    edge = edge_ref[...]

    def step(x, packed):
        row = RADIUS + x
        centers = [wide_ref[z, row] for z in range(planes)]
        plane_sum = (-0.5 * beta) * sum(centers)
        later = []
        for z in range(planes):
            own = own_ref[z, x]
            beside = pltpu.roll(edges_ref[1, z].astype(jnp.float32), y_cells - (x + 1) * RADIUS, 1)
            along_y = jnp.dot(
                jnp.concatenate([own, beside.astype(jnp.bfloat16)], 1), along, preferred_element_type=jnp.float32
            )
            total = plane_sum + (potential_ref[z, x] + kappa) * centers[z]
            for offset in range(1, RADIUS + 1):
                total = total + (-0.5 * COEFFS[offset]) * (wide_ref[z, row + offset] + wide_ref[z, row - offset])
            total = total + (along_y[:, :y_cells] + along_y[:, y_cells:])
            applied_ref[z, x] = total.astype(jnp.bfloat16)
            outside = jnp.dot(own, edge, preferred_element_type=jnp.float32)
            outside = outside[:, :y_cells] + outside[:, y_cells:]
            later.append(packed[z] + pltpu.roll(outside, x * RADIUS, 1))
        return tuple(later)

    zero = jnp.zeros((bands, y_cells), jnp.float32)
    packed = lax.fori_loop(0, x_cells, step, (zero,) * planes)
    for z in range(planes):
        applied_ref[z, x_cells] = packed[z].astype(jnp.bfloat16)


def pair_blocks(own_ref, applied_ref, partner_ref):
    planes, slabs, bands, _ = own_ref.shape
    dims = (((1,), (1,)), ((), ()))

    def plane(z, sums):
        gram, ham = sums
        for x in range(0, slabs - 1, 2):
            pair = lambda ref: jnp.concatenate([ref[z, x], ref[z, x + 1]], 1)
            partner = pair(partner_ref)
            gram += lax.dot_general(pair(own_ref), partner, dims, preferred_element_type=jnp.float32)
            ham += lax.dot_general(pair(applied_ref), partner, dims, preferred_element_type=jnp.float32)
        ham += lax.dot_general(
            applied_ref[z, slabs - 1], partner_ref[z, slabs - 1], dims, preferred_element_type=jnp.float32
        )
        return gram, ham

    zero = jnp.zeros((bands, bands), jnp.float32)
    return lax.fori_loop(0, planes, plane, (zero, zero))


def first_kernel(
    own_ref, before_ref, after_ref, edges_ref, potential_ref, along_ref, edge_ref, partner_ref,
    applied_ref, out_ref, wide_ref,
):
    stencil(
        own_ref, before_ref, after_ref, edges_ref, potential_ref, along_ref, edge_ref, applied_ref, wide_ref
    )
    out_ref[0], out_ref[1] = pair_blocks(own_ref, applied_ref, partner_ref)


def second_kernel(norm_scale, own_ref, applied_ref, partner_ref, before_ref, out_ref):
    places, _, rows, bands = out_ref.shape
    gram, ham = pair_blocks(own_ref, applied_ref, partner_ref)
    for index, block in enumerate((before_ref[0], before_ref[1], gram, ham)):
        out_ref[:, index] = (block * norm_scale).reshape(places, rows, bands)


def finish_kernel(direct_ref, mine_ref, theirs_ref, gram_ref, ham_ref):
    bands = mine_ref.shape[-1]
    for round_id in range(2):
        is_direct = direct_ref[round_id] == 1
        for kind, out_ref in enumerate((gram_ref, ham_ref)):
            mine = mine_ref[:, 2 * round_id + kind].reshape(bands, bands)
            theirs = theirs_ref[:, 2 * round_id + kind].reshape(bands, bands)
            direct = jnp.where(is_direct, mine, theirs)
            mirrored = jnp.where(is_direct, theirs, mine)
            out_ref[round_id] = direct + mirrored.T


def vmem(count):
    return [pl.BlockSpec(memory_space=pltpu.VMEM)] * count


def call(kernel, name, scalars, arrays, out_shapes, scratch=()):
    return pl.pallas_call(
        kernel,
        out_shape=out_shapes,
        in_specs=[pl.BlockSpec(memory_space=pltpu.SMEM)] * len(scalars) + vmem(len(arrays)),
        out_specs=vmem(1)[0] if not isinstance(out_shapes, list) else vmem(len(out_shapes)),
        scratch_shapes=list(scratch),
        compiler_params=pltpu.CompilerParams(vmem_limit_bytes=VMEM_LIMIT),
        name=name,
    )(*scalars, *arrays)


def body(orbitals, potential, pair_masks):
    bands, planes, x_cells, y_cells = orbitals.shape
    tx_count = lax.axis_size("tx")
    group = lax.axis_index("band")
    side = lax.axis_index("ty")
    norm_scale = float(planes * x_cells * y_cells * tx_count * SIDES) ** -0.5
    other_side = [(0, 1), (1, 0)]
    shape = lambda *sizes, dtype=jnp.float32: jax.ShapeDtypeStruct(sizes, dtype)

    slabs = shape(planes, x_cells + 1, bands, y_cells, dtype=jnp.bfloat16)
    message, head, tail, edges = prepare(orbitals)
    edges = lax.ppermute(edges, "ty", other_side)
    masks = [pair_masks[0] - 1, pair_masks[1] - 1]
    message, *masks = lax.optimization_barrier((message, *masks))
    message = lax.dynamic_update_slice(message, edges[0][:, None], (0, x_cells, 0, 0))
    before = lax.ppermute(tail, "tx", [(i, (i + 1) % tx_count) for i in range(tx_count)])
    after = lax.ppermute(head, "tx", [((i + 1) % tx_count, i) for i in range(tx_count)])

    first, later = first_by_mask(masks[0], message, masks[1])
    beside = lambda own, *others: call(
        first_kernel,
        "first",
        [],
        [own, *others],
        [pltpu.VMEM(slabs.shape, slabs.dtype), shape(2, bands, bands)],
        [pltpu.VMEM((planes, x_cells + 2 * RADIUS, bands, y_cells), jnp.float32)],
    )
    second, applied, first_blocks = second_by_mask(
        later,
        [
            message,
            before,
            after,
            edges,
            potential[:, :, None, :],
            jnp.asarray(along_matrix(y_cells)),
            jnp.asarray(before_matrix(y_cells)),
            first,
        ],
        beside,
    )
    partial_value = call(
        lambda *refs: second_kernel(norm_scale, *refs),
        "second",
        [],
        [message, applied, second, first_blocks],
        pltpu.VMEM((tx_count, 4, bands // tx_count, bands), jnp.float32),
    )
    total = jnp.sum(lax.all_to_all(partial_value, "tx", 0, 0), 0)
    held = jnp.concatenate(
        [
            total[2 * round_id : 2 * round_id + 2]
            + back_by_mask(masks[round_id], total[2 * round_id : 2 * round_id + 2])
            for round_id in range(2)
        ]
    )
    mine = lax.all_to_all(jnp.broadcast_to(held, (tx_count, *held.shape)), "tx", 0, 0)
    theirs = lax.ppermute(mine, "ty", other_side)
    lowest = jnp.bitwise_and(pair_masks, -pair_masks)
    received_on = (jnp.bitwise_and(lowest, group) != 0).astype(jnp.int32)
    direct = (received_on == side).astype(jnp.int32)
    block = shape(2, bands, bands)
    return call(finish_kernel, "finish", [direct], [mine, theirs], [block, block])


def solution(mesh):
    in_specs = (P("band", None, "tx", "ty"), P(None, "tx", "ty"), P())
    out_specs = (P(None, "band", None), P(None, "band", None))
    mapped = jax.shard_map(body, mesh=mesh, in_specs=in_specs, out_specs=out_specs, check_vma=False)
    return lambda *args: tuple(mapped(*args))
```

```python
import jax
import jax.numpy as jnp
import numpy as np
from jax import lax
from jax.experimental import pallas as pl
from jax.experimental.pallas import tpu as pltpu
from jax.sharding import PartitionSpec as P

COEFFS = (
    -5369.0 / 1800.0,
    12.0 / 7.0,
    -15.0 / 56.0,
    10.0 / 189.0,
    -1.0 / 112.0,
    2.0 / 1925.0,
    -1.0 / 16632.0,
)
RADIUS = 6
GROUPS = 16
SIDES = 2
VMEM_LIMIT = 40 * 2**20


def receiving_side(mask, group):
    return 1 if group & (mask & -mask) else 0


def sends(mask):
    return [
        (group * SIDES + side, (group ^ mask) * SIDES + side)
        for group in range(GROUPS)
        for side in range(SIDES)
        if receiving_side(mask, group) != side
    ]


def relays(change):
    return [
        (group * SIDES + (group & 1), (group ^ change) * SIDES + (group & 1)) for group in range(GROUPS)
    ]


RELAYED = (4, 8)


def first_by_mask(index, value, next_index):
    def branch(mask):
        def run(held, following):
            received = lax.ppermute(held, ("band", "ty"), sends(mask))
            chosen = following
            if mask & 1:
                for place, change in enumerate(RELAYED):
                    chosen = jnp.where(following == (mask ^ change) - 1, GROUPS - 1 + place, chosen)
            return received, chosen

        return run

    return lax.switch(index, [branch(mask) for mask in range(1, GROUPS)], value, next_index)


def second_by_mask(index, operands, beside):
    def branch(pairs, which):
        def run(*held):
            return lax.ppermute(held[which], ("band", "ty"), pairs), *beside(*held)

        return run

    branches = [branch(sends(mask), 0) for mask in range(1, GROUPS)]
    branches += [branch(relays(change), -1) for change in RELAYED]
    return lax.switch(index, branches, *operands)


def back_by_mask(index, value):
    back = lambda mask: [(target, source) for source, target in sends(mask)]
    branch = lambda pairs: lambda held: lax.ppermute(held, ("band", "ty"), pairs)
    return lax.switch(index, [branch(back(mask)) for mask in range(1, GROUPS)], value)


def split(matrix):
    high = matrix.astype(jnp.bfloat16)
    low = (matrix - high.astype(np.float64)).astype(jnp.bfloat16)
    return np.concatenate([high, low], 1)


def along_matrix(cells):
    matrix = np.zeros((2 * cells, cells), np.float64)
    for cell in range(cells):
        for offset in range(1, RADIUS + 1):
            matrix[cell + offset, cell] += -0.5 * COEFFS[offset]
            if cell >= offset:
                matrix[cell - offset, cell] += -0.5 * COEFFS[offset]
    return split(matrix)


def before_matrix(cells):
    matrix = np.zeros((cells, cells), np.float64)
    for place in range(RADIUS):
        for cell in range(place + 1):
            matrix[cell, place] = -0.5 * COEFFS[RADIUS - place + cell]
    return split(matrix)


def prepare_kernel(orbitals_ref, message_ref, head_ref, tail_ref, edges_ref):
    bands, _, x_cells, y_cells = orbitals_ref.shape
    lane = lax.broadcasted_iota(jnp.int32, (bands, y_cells), 1)
    message_ref[0, :x_cells] = jnp.swapaxes(orbitals_ref[:, 0], 0, 1)
    head_ref[0] = message_ref[0, :RADIUS]
    tail_ref[0] = message_ref[0, x_cells - RADIUS : x_cells]
    last = jnp.zeros((bands, y_cells), jnp.float32)
    first = last
    for x in range(x_cells):
        moved = pltpu.roll(message_ref[0, x].astype(jnp.float32), (x + 1) * RADIUS, 1)
        cell = lane - x * RADIUS
        last = jnp.where((cell >= 0) & (cell < RADIUS), moved, last)
        first = jnp.where((cell >= RADIUS) & (cell < 2 * RADIUS), moved, first)
    edges_ref[0, 0] = last.astype(jnp.bfloat16)
    edges_ref[1, 0] = first.astype(jnp.bfloat16)
    message_ref[0, x_cells] = jnp.zeros((bands, y_cells), jnp.bfloat16)


def prepare(orbitals):
    bands, planes, x_cells, y_cells = orbitals.shape
    plane = lambda *lead: pl.BlockSpec((1, *lead, bands, y_cells), lambda z: (z, *[0] * (len(lead) + 2)))
    array = lambda *lead: jax.ShapeDtypeStruct((*lead, bands, y_cells), jnp.bfloat16)
    return pl.pallas_call(
        prepare_kernel,
        grid=(planes,),
        in_specs=[pl.BlockSpec((bands, 1, x_cells, y_cells), lambda z: (0, z, 0, 0))],
        out_specs=[
            plane(x_cells + 1),
            plane(RADIUS),
            plane(RADIUS),
            pl.BlockSpec((2, 1, bands, y_cells), lambda z: (0, z, 0, 0)),
        ],
        out_shape=[array(planes, x_cells + 1), array(planes, RADIUS), array(planes, RADIUS), array(2, planes)],
        compiler_params=pltpu.CompilerParams(vmem_limit_bytes=VMEM_LIMIT),
        name="prepare",
    )(orbitals)


def stencil(own_ref, before_ref, after_ref, edges_ref, potential_ref, along_ref, edge_ref, applied_ref, wide_ref):
    planes, slabs, bands, y_cells = own_ref.shape
    x_cells = slabs - 1
    beta = COEFFS[1] + COEFFS[2] + COEFFS[4] + COEFFS[5]
    kappa = -0.5 * (3.0 * COEFFS[0] + 2.0 * COEFFS[3] + 2.0 * COEFFS[6] - beta)

    def widen(x, carry):
        for z in range(planes):
            wide_ref[z, RADIUS + x] = own_ref[z, x].astype(jnp.float32)
        return carry

    def widen_sides(x, carry):
        for z in range(planes):
            wide_ref[z, x] = before_ref[z, x].astype(jnp.float32)
            wide_ref[z, RADIUS + x_cells + x] = after_ref[z, x].astype(jnp.float32)
        return carry

    lax.fori_loop(0, x_cells, widen, 0)
    lax.fori_loop(0, RADIUS, widen_sides, 0)
    along = along_ref[...]
    edge = edge_ref[...]

    def step(x, packed):
        row = RADIUS + x
        centers = [wide_ref[z, row] for z in range(planes)]
        plane_sum = (-0.5 * beta) * sum(centers)
        later = []
        for z in range(planes):
            own = own_ref[z, x]
            beside = pltpu.roll(edges_ref[1, z].astype(jnp.float32), y_cells - (x + 1) * RADIUS, 1)
            along_y = jnp.dot(
                jnp.concatenate([own, beside.astype(jnp.bfloat16)], 1), along, preferred_element_type=jnp.float32
            )
            total = plane_sum + (potential_ref[z, x] + kappa) * centers[z]
            for offset in range(1, RADIUS + 1):
                total = total + (-0.5 * COEFFS[offset]) * (wide_ref[z, row + offset] + wide_ref[z, row - offset])
            total = total + (along_y[:, :y_cells] + along_y[:, y_cells:])
            applied_ref[z, x] = total.astype(jnp.bfloat16)
            outside = jnp.dot(own, edge, preferred_element_type=jnp.float32)
            outside = outside[:, :y_cells] + outside[:, y_cells:]
            later.append(packed[z] + pltpu.roll(outside, x * RADIUS, 1))
        return tuple(later)

    zero = jnp.zeros((bands, y_cells), jnp.float32)
    packed = lax.fori_loop(0, x_cells, step, (zero,) * planes)
    for z in range(planes):
        applied_ref[z, x_cells] = packed[z].astype(jnp.bfloat16)


def pair_blocks(own_ref, applied_ref, partner_ref):
    planes, slabs, bands, _ = own_ref.shape
    dims = (((1,), (1,)), ((), ()))

    def plane(z, sums):
        gram, ham = sums
        for x in range(0, slabs - 1, 2):
            pair = lambda ref: jnp.concatenate([ref[z, x], ref[z, x + 1]], 1)
            partner = pair(partner_ref)
            gram += lax.dot_general(pair(own_ref), partner, dims, preferred_element_type=jnp.float32)
            ham += lax.dot_general(pair(applied_ref), partner, dims, preferred_element_type=jnp.float32)
        ham += lax.dot_general(
            applied_ref[z, slabs - 1], partner_ref[z, slabs - 1], dims, preferred_element_type=jnp.float32
        )
        return gram, ham

    zero = jnp.zeros((bands, bands), jnp.float32)
    return lax.fori_loop(0, planes, plane, (zero, zero))


def first_kernel(
    own_ref, before_ref, after_ref, edges_ref, potential_ref, along_ref, edge_ref, partner_ref,
    applied_ref, out_ref, wide_ref,
):
    stencil(
        own_ref, before_ref, after_ref, edges_ref, potential_ref, along_ref, edge_ref, applied_ref, wide_ref
    )
    out_ref[0], out_ref[1] = pair_blocks(own_ref, applied_ref, partner_ref)


def second_kernel(norm_scale, own_ref, applied_ref, partner_ref, before_ref, out_ref):
    places, _, rows, bands = out_ref.shape
    gram, ham = pair_blocks(own_ref, applied_ref, partner_ref)
    for index, block in enumerate((before_ref[0], before_ref[1], gram, ham)):
        out_ref[:, index] = (block * norm_scale).reshape(places, rows, bands)


def finish_kernel(direct_ref, order_ref, mine_ref, theirs_ref, gram_ref, ham_ref):
    bands = mine_ref.shape[-1]
    for round_id in range(2):
        is_direct = direct_ref[round_id] == 1
        for kind, out_ref in enumerate((gram_ref, ham_ref)):
            mine = mine_ref[:, 2 * round_id + kind].reshape(bands, bands)
            theirs = theirs_ref[:, 2 * round_id + kind].reshape(bands, bands)
            direct = jnp.where(is_direct, mine, theirs)
            mirrored = jnp.where(is_direct, theirs, mine)
            out_ref[round_id ^ order_ref[0]] = direct + mirrored.T


def vmem(count):
    return [pl.BlockSpec(memory_space=pltpu.VMEM)] * count


def call(kernel, name, scalars, arrays, out_shapes, scratch=()):
    return pl.pallas_call(
        kernel,
        out_shape=out_shapes,
        in_specs=[pl.BlockSpec(memory_space=pltpu.SMEM)] * len(scalars) + vmem(len(arrays)),
        out_specs=vmem(1)[0] if not isinstance(out_shapes, list) else vmem(len(out_shapes)),
        scratch_shapes=list(scratch),
        compiler_params=pltpu.CompilerParams(vmem_limit_bytes=VMEM_LIMIT),
        name=name,
    )(*scalars, *arrays)


def body(orbitals, potential, pair_masks):
    bands, planes, x_cells, y_cells = orbitals.shape
    tx_count = lax.axis_size("tx")
    group = lax.axis_index("band")
    side = lax.axis_index("ty")
    norm_scale = float(planes * x_cells * y_cells * tx_count * SIDES) ** -0.5
    other_side = [(0, 1), (1, 0)]
    shape = lambda *sizes, dtype=jnp.float32: jax.ShapeDtypeStruct(sizes, dtype)

    slabs = shape(planes, x_cells + 1, bands, y_cells, dtype=jnp.bfloat16)
    message, head, tail, edges = prepare(orbitals)
    edges = lax.ppermute(edges, "ty", other_side)
    swap = jnp.bitwise_and(pair_masks[0], 3) == 2
    masks = [
        jnp.where(swap, pair_masks[1], pair_masks[0]) - 1,
        jnp.where(swap, pair_masks[0], pair_masks[1]) - 1,
    ]
    message, *masks = lax.optimization_barrier((message, *masks))
    message = lax.dynamic_update_slice(message, edges[0][:, None], (0, x_cells, 0, 0))
    before = lax.ppermute(tail, "tx", [(i, (i + 1) % tx_count) for i in range(tx_count)])
    after = lax.ppermute(head, "tx", [((i + 1) % tx_count, i) for i in range(tx_count)])

    first, later = first_by_mask(masks[0], message, masks[1])
    beside = lambda own, *others: call(
        first_kernel,
        "first",
        [],
        [own, *others],
        [pltpu.VMEM(slabs.shape, slabs.dtype), shape(2, bands, bands)],
        [pltpu.VMEM((planes, x_cells + 2 * RADIUS, bands, y_cells), jnp.float32)],
    )
    second, applied, first_blocks = second_by_mask(
        later,
        [
            message,
            before,
            after,
            edges,
            potential[:, :, None, :],
            jnp.asarray(along_matrix(y_cells)),
            jnp.asarray(before_matrix(y_cells)),
            first,
        ],
        beside,
    )
    partial_value = call(
        lambda *refs: second_kernel(norm_scale, *refs),
        "second",
        [],
        [message, applied, second, first_blocks],
        pltpu.VMEM((tx_count, 4, bands // tx_count, bands), jnp.float32),
    )
    total = jnp.sum(lax.all_to_all(partial_value, "tx", 0, 0), 0)
    held = jnp.concatenate(
        [
            total[2 * round_id : 2 * round_id + 2]
            + back_by_mask(masks[round_id], total[2 * round_id : 2 * round_id + 2])
            for round_id in range(2)
        ]
    )
    mine = lax.all_to_all(jnp.broadcast_to(held, (tx_count, *held.shape)), "tx", 0, 0)
    theirs = lax.ppermute(mine, "ty", other_side)
    sent = jnp.stack(masks) + 1
    lowest = jnp.bitwise_and(sent, -sent)
    received_on = (jnp.bitwise_and(lowest, group) != 0).astype(jnp.int32)
    direct = (received_on == side).astype(jnp.int32)
    block = shape(2, bands, bands)
    order = jnp.where(swap, 1, 0).astype(jnp.int32)[None]
    return call(finish_kernel, "finish", [direct, order], [mine, theirs], [block, block])


def solution(mesh):
    in_specs = (P("band", None, "tx", "ty"), P(None, "tx", "ty"), P())
    out_specs = (P(None, "band", None), P(None, "band", None))
    mapped = jax.shard_map(body, mesh=mesh, in_specs=in_specs, out_specs=out_specs, check_vma=False)
    return lambda *args: tuple(mapped(*args))
```
